32 devices in a mesh: lat: 4 (over y, x), ang: 8 (over z, core).
Axes of the slice: x: 2, y: 2, z: 4, core: 2. Of those that a mesh axis runs over, the one named last changes fastest.
Arguments:
- incident: float32 [2, 256, 131072], P(None, 'ang', 'lat'), may hold values from -6 to 6
- detuning: float32 [256], P('ang'), may hold values from -1.5 to 1.5
- phase_table: int32 [3, 131072], P(None, 'lat'), may hold values from -32768 to 32767
- response: float32 [256, 256], replicated, may hold values from 0 to 2, as said below
- counts: int32 [256, 131072], P(None, ('lat', 'ang')), may hold values from 0 to 3
Outputs:
- exit_field: float32 [2, 256, 131072], P(None, 'ang', 'lat')
- estimate: float32 [256, 131072], P('ang', 'lat')
The draws below stay inside these ranges and needn't reach their ends.
Inputs may be any that keep to these rules, and one draw needn't show every extreme that they name: `response`: every entry is positive.
All inputs are finite; a program needn't handle non-finite values.
Results may differ from the reference program's by a relative error of at most 0.00013.
Values sent between devices are 32-bit elements; how exact they have to be, the bound alone decides.
A program may use at most 128 MiB of HBM per device.

```python
import math
import jax
import jax.numpy as jnp
from jax import lax

COLS = 512
ANGLES = 256
BLOCKS = 3
STEPS = 3
ITERS = 6
NPOINTS = 131072


def draw_response(key, part):
    key_diagonal = jax.random.fold_in(key, 11)
    key_band = jax.random.fold_in(key, 12)
    band_width = ANGLES // 8
    angle_index = jnp.arange(ANGLES)
    distance = jnp.abs(angle_index[:, None] - angle_index[None, :]).astype(jnp.float32)
    roughness = jax.random.uniform(key_band, (ANGLES, ANGLES), jnp.float32, 0.05, 1.0)
    diagonal_part = jax.random.uniform(key_diagonal, (ANGLES,), jnp.float32, 0.3, 0.6)
    banded = roughness * jnp.exp(-distance / band_width) * (0.5 / band_width)
    return banded + jnp.diag(diagonal_part)


def place_ends(result, stream_key, low, high):
    index_at = [jax.random.randint(jax.random.fold_in(stream_key, axis), (), 0, length) for axis, length in enumerate(result.shape)]
    main_axis = result.shape.index(max(result.shape))
    neighbour = index_at[:main_axis] + [(index_at[main_axis] + 1) % result.shape[main_axis]] + index_at[main_axis + 1:]
    return result.at[tuple(index_at)].set(low).at[tuple(neighbour)].set(high)


def block_scale(key, dims, split, least, largest):
    level, own = 1.0, jax.random.fold_in(key, 6)
    for position, parts in split:
        steps = jnp.exp(jax.random.uniform(jax.random.fold_in(own, position), (parts,), jnp.float32, least / len(split), largest / len(split)))
        level = level * jnp.repeat(steps, dims[position] // parts).reshape([-1 if axis == position else 1 for axis in range(len(dims))])
    return level


def scatter_about(stream_key, extent, deviation, reach, pieces=(), held_as=jnp.bfloat16):
    values = jax.random.normal(stream_key, extent, jnp.float32) * deviation
    if len(pieces) > 0:
        values = block_scale(stream_key, extent, pieces, -0.22, 0.18) * values
    return jnp.clip(values, min=-reach, max=reach).astype(held_as)


def setup_inputs(seed: int = 0) -> dict:
    key_list = jax.random.split(jax.random.key(seed), 6)
    incident = scatter_about(key_list[0], (2, ANGLES, NPOINTS), 1.0, 6.0, ((1, 8), (2, 4)), jnp.float32)
    detuning = jnp.clip(jax.random.uniform(key_list[1], (ANGLES,), jnp.float32, -1.5, 1.5) * block_scale(key_list[1], (ANGLES,), ((0, 8),), -0.4, 0.0), -1.5, 1.5)
    phase_table = place_ends(jax.random.randint(key_list[2], (BLOCKS, NPOINTS), -32768, 32768), jax.random.fold_in(key_list[2], 1), -32768, 32767).astype(jnp.int32)
    response = draw_response(jax.random.fold_in(key_list[5], 71), 0)
    counts = place_ends(jax.random.randint(key_list[4], (ANGLES, NPOINTS), 0, 4), jax.random.fold_in(key_list[4], 1), 0, 3).astype(jnp.int32)
    return dict(incident=incident, detuning=detuning, phase_table=phase_table, response=response, counts=counts)


coupling = 0.6
background = 0.25
phase_unit = math.pi / 32768.0


def rotate(beam_real, beam_imag, bragg_real, bragg_imag, phase_cos, phase_sin, detune_cos, detune_sin):
    cos_kappa = math.cos(coupling)
    sin_kappa = math.sin(coupling)
    mixed_real = phase_cos * bragg_real + phase_sin * bragg_imag
    mixed_imag = phase_cos * bragg_imag - phase_sin * bragg_real
    ahead_real = cos_kappa * beam_real - sin_kappa * mixed_imag
    ahead_imag = cos_kappa * beam_imag + sin_kappa * mixed_real
    driven_real = phase_cos * beam_real - phase_sin * beam_imag
    driven_imag = phase_cos * beam_imag + phase_sin * beam_real
    inner_real = cos_kappa * bragg_real - sin_kappa * driven_imag
    inner_imag = cos_kappa * bragg_imag + sin_kappa * driven_real
    out_real = detune_cos * inner_real + detune_sin * inner_imag
    out_imag = detune_cos * inner_imag - detune_sin * inner_real
    return ahead_real, ahead_imag, out_real, out_imag


def reference(incident, detuning, phase_table, response, counts):
    detune_cos = jnp.cos(detuning)[:, None]
    detune_sin = jnp.sin(detuning)[:, None]
    beam_real = incident[0]
    beam_imag = incident[1]
    bragg_real = jnp.zeros_like(beam_real)
    bragg_imag = jnp.zeros_like(beam_real)
    for block_index in range(BLOCKS):
        phase_angle = phase_table[block_index].astype(jnp.float32) * phase_unit
        phase_cos = jnp.cos(phase_angle)[None, :]
        phase_sin = jnp.sin(phase_angle)[None, :]
        for step_index in range(STEPS):
            turned = rotate(beam_real, beam_imag, bragg_real, bragg_imag, phase_cos, phase_sin, detune_cos, detune_sin)
            beam_real = jnp.roll(turned[0], COLS, axis=1)
            beam_imag = jnp.roll(turned[1], COLS, axis=1)
            bragg_real = jnp.roll(turned[2], -COLS, axis=1)
            bragg_imag = jnp.roll(turned[3], -COLS, axis=1)
    exit_field = jnp.stack([bragg_real, bragg_imag])
    estimate = bragg_real * bragg_real + bragg_imag * bragg_imag
    measured = counts.astype(jnp.float32)
    column_sums = jnp.sum(response, axis=0)[:, None]
    for iteration in range(ITERS):
        blurred = jnp.dot(response, estimate, precision=lax.Precision.HIGHEST, preferred_element_type=jnp.float32) + background
        projected = lax.dot_general(response, measured / blurred, (((0,), (0,)), ((), ())), precision=lax.Precision.HIGHEST, preferred_element_type=jnp.float32)
        estimate = estimate * projected / column_sums
    return exit_field, estimate
```

```python
import functools
import math

import jax
import jax.numpy as jnp
from jax import lax
from jax.experimental import pallas as pl
from jax.experimental.pallas import tpu as pltpu
from jax.sharding import PartitionSpec as P

COLS = 512
BLOCKS = 3
STEPS = 3
ITERS = 6
TOTAL = BLOCKS * STEPS
BEFORE = TOTAL - 2
AFTER = TOTAL
GROUP = 8

coupling = 0.6
background = 0.25
phase_unit = math.pi / 32768.0
tan_kappa = math.tan(coupling)
tan_squared = tan_kappa * tan_kappa
end_scale = math.cos(coupling) ** TOTAL / tan_kappa


def passed_along(x, axis, by):
    devices = lax.axis_size(axis)
    return lax.ppermute(x, axis, [(i, (i + by) % devices) for i in range(devices)])


def table_of(step):
    block, last = divmod(step, STEPS)
    return block + (BLOCKS if last == STEPS - 1 else 0)


def sweep_kernel(halves, dests, *refs):
    (inc, before, after, tab_cos, tab_sin, det_cos, det_sin) = refs[:7]
    exit_ref, int_ref, beam_re, beam_im, bragg_re, bragg_im = refs[-6:]
    span_rows = inc.shape[2] // COLS
    rows = span_rows + BEFORE + AFTER
    dcos = jnp.broadcast_to(det_cos[...], (GROUP, COLS))
    dsin = jnp.broadcast_to(det_sin[...], (GROUP, COLS))

    def at(k):
        return pl.ds(pl.multiple_of(k * COLS, COLS), COLS)

    def turned(re, im, table, row):
        pc = tab_cos[table, pl.ds(row, 1), :]
        ps = tab_sin[table, pl.ds(row, 1), :]
        a = dcos * re + dsin * im
        b = dcos * im - dsin * re
        return pc * a - ps * b, pc * b + ps * a

    def enter(source, count, shift):
        @pl.loop(0, count)
        def _(k):
            re = source[0, :, at(k)]
            im = source[1, :, at(k)]
            beam_re[:, at(k + shift)] = re
            beam_im[:, at(k + shift)] = im
            out_re, out_im = turned(-tan_squared * im, tan_squared * re, table_of(0), k + shift)
            bragg_re[:, at(k + shift)] = out_re
            bragg_im[:, at(k + shift)] = out_im

    enter(before, BEFORE, 0)
    enter(inc, span_rows, BEFORE)
    enter(after, AFTER, BEFORE + span_rows)

    for step in range(1, TOTAL - 1):

        @pl.loop(0, rows // 2 - step)
        def _(pair):
            for odd in range(2):
                k = pair * 2 + odd
                here, there = at(k), at(k + 2 * step)
                t_re, t_im = beam_re[:, here], beam_im[:, here]
                d_re, d_im = bragg_re[:, there], bragg_im[:, there]
                beam_re[:, here] = t_re - d_im
                beam_im[:, here] = t_im + d_re
                out_re, out_im = turned(
                    d_re - tan_squared * t_im, d_im + tan_squared * t_re, table_of(step), k + step
                )
                bragg_re[:, there] = out_re
                bragg_im[:, there] = out_im

    step = TOTAL - 1
    per_dest = span_rows // dests
    per_half = per_dest // halves

    @pl.loop(0, dests)
    def _(dest):
        for inner in range(per_dest):
            k = dest * per_dest + inner
            here, there = at(k), at(k + 2 * step)
            t_re, t_im = beam_re[:, here], beam_im[:, here]
            d_re, d_im = bragg_re[:, there], bragg_im[:, there]
            out_re, out_im = turned(
                d_re - tan_squared * t_im, d_im + tan_squared * t_re, table_of(step), k + step
            )
            exit_ref[0, :, here] = out_re
            exit_ref[1, :, here] = out_im
            half, place = divmod(inner, per_half)
            int_ref[half, dest, :, place * COLS : (place + 1) * COLS] = out_re * out_re + out_im * out_im


def sweep(group, halves, dests, incident, before, after, tab_cos, tab_sin, det_cos, det_sin, exit_field):
    _, angles, span = incident.shape
    rows = span // COLS + BEFORE + AFTER
    points = span // dests // halves
    whole = lambda x: pl.BlockSpec(x.shape, lambda i: (0,) * x.ndim)
    in_specs = [
        pl.BlockSpec((2, GROUP, span), lambda i: (0, group, 0)),
        whole(before),
        whole(after),
        whole(tab_cos),
        whole(tab_sin),
        pl.BlockSpec((GROUP, 1), lambda i: (group, 0)),
        pl.BlockSpec((GROUP, 1), lambda i: (group, 0)),
    ]
    operands = [incident, before, after, tab_cos, tab_sin, det_cos, det_sin]
    aliases = {}
    if exit_field is not None:
        in_specs.append(pl.BlockSpec(memory_space=pl.ANY))
        operands.append(exit_field)
        aliases = {7: 0}
    return pl.pallas_call(
        functools.partial(sweep_kernel, halves, dests),
        grid=(1,),
        out_shape=[
            jax.ShapeDtypeStruct((2, angles, span), jnp.float32),
            jax.ShapeDtypeStruct((halves, dests, GROUP, points), jnp.float32),
        ],
        in_specs=in_specs,
        out_specs=[
            pl.BlockSpec((2, GROUP, span), lambda i: (0, group, 0)),
            pl.BlockSpec((halves, dests, GROUP, points), lambda i: (0, 0, 0, 0)),
        ],
        scratch_shapes=[pltpu.VMEM((GROUP, rows * COLS), jnp.float32)] * 4,
        input_output_aliases=aliases,
        compiler_params=pltpu.CompilerParams(vmem_limit_bytes=40 * 1024 * 1024),
        cost_estimate=pl.CostEstimate(
            flops=20 * TOTAL * GROUP * rows * COLS,
            bytes_accessed=28 * GROUP * span,
            transcendentals=0,
        ),
    )(*operands)


def phase_tables(phase_table, span):
    before = passed_along(phase_table[:, span - BEFORE * COLS :], "lat", 1)
    after = passed_along(phase_table[:, : AFTER * COLS], "lat", -1)
    phase = jnp.concatenate([before, phase_table, after], axis=1).reshape(BLOCKS, -1, COLS)
    earlier = jnp.roll(phase, 1, axis=1)
    leaving = jnp.concatenate([earlier[1:], jnp.zeros_like(phase[:1])], axis=0)
    turns = jnp.concatenate([phase - earlier, phase - leaving], axis=0)
    angle = turns.astype(jnp.float32) * phase_unit
    scale = jnp.ones((2 * BLOCKS, 1, 1), jnp.float32).at[2 * BLOCKS - 1].set(end_scale)
    return jnp.cos(angle) * scale, jnp.sin(angle) * scale


def deconvolve(response, backward, estimate, counts):
    measured = counts.astype(jnp.float32)
    for _ in range(ITERS):
        blurred = (
            jnp.dot(
                response,
                estimate,
                precision=lax.Precision.HIGH,
                preferred_element_type=jnp.float32,
            )
            + background
        )
        projected = lax.dot_general(
            backward,
            measured / blurred,
            (((0,), (0,)), ((), ())),
            precision=lax.Precision.HIGH,
            preferred_element_type=jnp.float32,
        )
        estimate = estimate * projected
    return estimate


def on_device(incident, detuning, phase_table, response, counts):
    _, angles, span = incident.shape
    dests = lax.axis_size("ang")
    points = span // dests
    halves = 2 if (points // COLS) % 2 == 0 else 1
    part = points // halves
    groups = angles // GROUP

    halos = []
    for group in range(groups):
        mine = incident[:, group * GROUP : (group + 1) * GROUP]
        halos.append(
            (
                passed_along(mine[:, :, span - BEFORE * COLS :], "lat", 1),
                passed_along(mine[:, :, : AFTER * COLS], "lat", -1),
            )
        )
    tab_cos, tab_sin = phase_tables(phase_table, span)
    det_cos = jnp.cos(detuning)[:, None]
    det_sin = jnp.sin(detuning)[:, None]

    def exchanged(x):
        return lax.all_to_all(x, "ang", split_axis=0, concat_axis=0, tiled=True)

    exit_field = None
    intensity = []
    for group in range(groups):
        exit_field, made = sweep(
            group, halves, dests, incident, *halos[group], tab_cos, tab_sin, det_cos, det_sin, exit_field
        )
        intensity.append(made)
    early = groups // 2
    arrived = [[exchanged(made[half]) for half in range(halves)] for made in intensity[:early]]
    late = [
        exchanged(jnp.concatenate([made[half] for made in intensity[early:]], axis=1))
        for half in range(halves)
    ]
    backward = response / jnp.sum(response, axis=0)[None, :]
    returned = []
    for half in range(halves):
        start = jnp.concatenate([a[half] for a in arrived] + [late[half]], axis=1)
        estimate = deconvolve(
            response,
            backward,
            start.reshape(dests * angles, part),
            counts[:, half * part : (half + 1) * part],
        )
        returned.append(exchanged(estimate.reshape(dests, angles, part)))
    placed = jnp.stack(returned, axis=0).transpose(2, 1, 0, 3).reshape(angles, span)
    return (exit_field, placed)


def solution(mesh):
    return jax.shard_map(
        on_device,
        mesh=mesh,
        in_specs=(P(None, "ang", "lat"), P("ang"), P(None, "lat"), P(), P(None, ("lat", "ang"))),
        out_specs=(P(None, "ang", "lat"), P("ang", "lat")),
        check_vma=False,
    )
```

```python
import functools
import math

import jax
import jax.numpy as jnp
from jax import lax
from jax.experimental import pallas as pl
from jax.experimental.pallas import tpu as pltpu
from jax.sharding import PartitionSpec as P

COLS = 512
BLOCKS = 3
STEPS = 3
ITERS = 6
TOTAL = BLOCKS * STEPS
BEFORE = TOTAL - 2
AFTER = TOTAL
GROUP = 8

coupling = 0.6
background = 0.25
phase_unit = math.pi / 32768.0
tan_kappa = math.tan(coupling)
tan_squared = tan_kappa * tan_kappa
end_scale = math.cos(coupling) ** TOTAL / tan_kappa


def passed_along(x, axis, by):
    devices = lax.axis_size(axis)
    return lax.ppermute(x, axis, [(i, (i + by) % devices) for i in range(devices)])


def table_of(step):
    block, last = divmod(step, STEPS)
    return block + (BLOCKS if last == STEPS - 1 else 0)


def sweep_kernel(halves, dests, *refs):
    (inc, before, after, tab_cos, tab_sin, det_cos, det_sin) = refs[:7]
    exit_ref, *int_refs = refs[-5 - halves : -4]
    beam_re, beam_im, bragg_re, bragg_im = refs[-4:]
    span_rows = inc.shape[2] // COLS
    rows = span_rows + BEFORE + AFTER
    dcos = jnp.broadcast_to(det_cos[...], (GROUP, COLS))
    dsin = jnp.broadcast_to(det_sin[...], (GROUP, COLS))

    def at(k):
        return pl.ds(pl.multiple_of(k * COLS, COLS), COLS)

    def turned(re, im, table, row):
        pc = tab_cos[table, pl.ds(row, 1), :]
        ps = tab_sin[table, pl.ds(row, 1), :]
        a = dcos * re + dsin * im
        b = dcos * im - dsin * re
        return pc * a - ps * b, pc * b + ps * a

    def enter(source, count, shift):
        @pl.loop(0, count)
        def _(k):
            re = source[0, :, at(k)]
            im = source[1, :, at(k)]
            beam_re[:, at(k + shift)] = re
            beam_im[:, at(k + shift)] = im
            out_re, out_im = turned(-tan_squared * im, tan_squared * re, table_of(0), k + shift)
            bragg_re[:, at(k + shift)] = out_re
            bragg_im[:, at(k + shift)] = out_im

    enter(before, BEFORE, 0)
    enter(inc, span_rows, BEFORE)
    enter(after, AFTER, BEFORE + span_rows)

    for step in range(1, TOTAL - 1):

        @pl.loop(0, rows // 2 - step)
        def _(pair):
            for odd in range(2):
                k = pair * 2 + odd
                here, there = at(k), at(k + 2 * step)
                t_re, t_im = beam_re[:, here], beam_im[:, here]
                d_re, d_im = bragg_re[:, there], bragg_im[:, there]
                beam_re[:, here] = t_re - d_im
                beam_im[:, here] = t_im + d_re
                out_re, out_im = turned(
                    d_re - tan_squared * t_im, d_im + tan_squared * t_re, table_of(step), k + step
                )
                bragg_re[:, there] = out_re
                bragg_im[:, there] = out_im

    step = TOTAL - 1
    per_dest = span_rows // dests
    per_half = per_dest // halves

    @pl.loop(0, dests)
    def _(dest):
        for inner in range(per_dest):
            k = dest * per_dest + inner
            here, there = at(k), at(k + 2 * step)
            t_re, t_im = beam_re[:, here], beam_im[:, here]
            d_re, d_im = bragg_re[:, there], bragg_im[:, there]
            out_re, out_im = turned(
                d_re - tan_squared * t_im, d_im + tan_squared * t_re, table_of(step), k + step
            )
            exit_ref[0, :, here] = out_re
            exit_ref[1, :, here] = out_im
            half, place = divmod(inner, per_half)
            int_refs[half][dest, :, place * COLS : (place + 1) * COLS] = out_re * out_re + out_im * out_im


def sweep(group, halo, first, halves, dests, count, incident, tables, detune, exit_field, made):
    _, angles, span = incident.shape
    before, after = halo
    rows = span // COLS + BEFORE + AFTER
    points = span // dests // halves
    place = 0 if made is None else made[0]
    whole = lambda x: pl.BlockSpec(x.shape, lambda i: (0,) * x.ndim)
    in_specs = [
        pl.BlockSpec((2, GROUP, span), lambda i: (0, group, 0)),
        pl.BlockSpec((2, GROUP, before.shape[2]), lambda i: (0, group - first, 0)),
        pl.BlockSpec((2, GROUP, after.shape[2]), lambda i: (0, group - first, 0)),
        whole(tables[0]),
        whole(tables[1]),
        pl.BlockSpec((GROUP, 1), lambda i: (group, 0)),
        pl.BlockSpec((GROUP, 1), lambda i: (group, 0)),
    ]
    operands = [incident, before, after, *tables, *detune]
    aliases = {}
    kept = ([] if exit_field is None else [(0, exit_field)]) + (
        [] if made is None else [(1 + half, x) for half, x in enumerate(made[1])]
    )
    for out, x in kept:
        aliases[len(operands)] = out
        in_specs.append(pl.BlockSpec(memory_space=pl.ANY))
        operands.append(x)
    exit_field, *made = pl.pallas_call(
        functools.partial(sweep_kernel, halves, dests),
        grid=(1,),
        out_shape=[jax.ShapeDtypeStruct((2, angles, span), jnp.float32)]
        + [jax.ShapeDtypeStruct((dests, count * GROUP, points), jnp.float32)] * halves,
        in_specs=in_specs,
        out_specs=[pl.BlockSpec((2, GROUP, span), lambda i: (0, group, 0))]
        + [pl.BlockSpec((dests, GROUP, points), lambda i: (0, place, 0))] * halves,
        scratch_shapes=[pltpu.VMEM((GROUP, rows * COLS), jnp.float32)] * 4,
        input_output_aliases=aliases,
        compiler_params=pltpu.CompilerParams(vmem_limit_bytes=40 * 1024 * 1024),
        cost_estimate=pl.CostEstimate(
            flops=20 * TOTAL * GROUP * rows * COLS,
            bytes_accessed=20 * GROUP * span,
            transcendentals=0,
        ),
    )(*operands)
    return exit_field, (place + 1, made)


def place_kernel(source, *refs):
    refs[-1][...] = source[0]


def placed(half, halves, x, whole):
    dests, angles, part = x.shape
    kept = [] if whole is None else [whole]
    return pl.pallas_call(
        place_kernel,
        grid=(dests,),
        out_shape=jax.ShapeDtypeStruct((angles, dests * halves * part), jnp.float32),
        in_specs=[pl.BlockSpec((1, angles, part), lambda i: (i, 0, 0))]
        + [pl.BlockSpec(memory_space=pl.ANY)] * len(kept),
        out_specs=pl.BlockSpec((angles, part), lambda i: (0, i * halves + half)),
        input_output_aliases={1: 0} if kept else {},
        cost_estimate=pl.CostEstimate(flops=0, bytes_accessed=8 * x.size, transcendentals=0),
    )(x, *kept)


def phase_tables(phase):
    earlier = jnp.roll(phase, 1, axis=1)
    leaving = jnp.concatenate([earlier[1:], jnp.zeros_like(phase[:1])], axis=0)
    turns = jnp.concatenate([phase - earlier, phase - leaving], axis=0)
    angle = turns * phase_unit
    scale = jnp.ones((2 * BLOCKS, 1, 1), jnp.float32).at[2 * BLOCKS - 1].set(end_scale)
    return jnp.cos(angle) * scale, jnp.sin(angle) * scale


def deconvolve(response, backward, estimate, counts):
    measured = counts.astype(jnp.float32)
    for _ in range(ITERS):
        blurred = (
            jnp.dot(
                response,
                estimate,
                precision=lax.Precision.HIGH,
                preferred_element_type=jnp.float32,
            )
            + background
        )
        projected = lax.dot_general(
            backward,
            measured / blurred,
            (((0,), (0,)), ((), ())),
            precision=lax.Precision.HIGH,
            preferred_element_type=jnp.float32,
        )
        estimate = estimate * projected
    return estimate


def on_device(incident, detuning, phase_table, response, counts):
    _, angles, span = incident.shape
    dests = lax.axis_size("ang")
    points = span // dests
    halves = 2 if (points // COLS) % 2 == 0 else 1
    part = points // halves
    groups = angles // GROUP

    def neighbours(x):
        return (
            passed_along(x[..., span - BEFORE * COLS :], "lat", 1),
            passed_along(x[..., : AFTER * COLS], "lat", -1),
        )

    def exchanged(x):
        return lax.all_to_all(x, "ang", split_axis=0, concat_axis=0, tiled=True)

    phase = phase_table.astype(jnp.float32)
    ends = (slice(span - BEFORE * COLS, span), slice(0, AFTER * COLS))
    before, after = (
        passed_along(
            jnp.concatenate([incident[0, :GROUP, end], incident[1, :GROUP, end], phase[:, end]]), "lat", by
        )
        for end, by in zip(ends, (1, -1))
    )
    phase = jnp.concatenate([before[2 * GROUP :], phase, after[2 * GROUP :]], axis=1)
    tables = phase_tables(phase.reshape(BLOCKS, -1, COLS))
    halos = {0: (0, tuple(x[: 2 * GROUP].reshape(2, GROUP, -1) for x in (before, after)))}
    group = 1
    while group < groups:
        count = 1 if group == 1 else groups - group
        halo = neighbours(incident[:, group * GROUP : (group + count) * GROUP])
        for one in range(group, group + count):
            halos[one] = (group, halo)
        group += count
    detune = (jnp.cos(detuning)[:, None], jnp.sin(detuning)[:, None])

    exit_field, (_, made) = sweep(
        0, halos[0][1], 0, 1, dests, 1, incident, tables, detune, None, None
    )
    early = exchanged(made[0])
    late = []
    if groups > 1:
        made = None
        for group in range(1, groups):
            first, halo = halos[group]
            exit_field, made = sweep(
                group, halo, first, halves, dests, groups - 1, incident, tables, detune, exit_field, made
            )
        for half in range(halves):
            late.append(exchanged(made[1][half]))
    backward = response / jnp.sum(response, axis=0)[None, :]
    whole = None
    for half in range(halves):
        start = jnp.concatenate(
            [early[:, :, half * part : (half + 1) * part]] + late[half : half + 1], axis=1
        )
        early, start = lax.optimization_barrier((early, start))
        estimate = deconvolve(
            response,
            backward,
            start.reshape(dests * angles, part),
            counts[:, half * part : (half + 1) * part],
        )
        whole = placed(half, halves, exchanged(estimate.reshape(dests, angles, part)), whole)
    return (exit_field, whole)


def solution(mesh):
    return jax.shard_map(
        on_device,
        mesh=mesh,
        in_specs=(P(None, "ang", "lat"), P("ang"), P(None, "lat"), P(), P(None, ("lat", "ang"))),
        out_specs=(P(None, "ang", "lat"), P("ang", "lat")),
        check_vma=False,
    )
```

```python
import functools
import math

import jax
import jax.numpy as jnp
from jax import lax
from jax.experimental import pallas as pl
from jax.experimental.pallas import tpu as pltpu
from jax.sharding import PartitionSpec as P

COLS = 512
BLOCKS = 3
STEPS = 3
ITERS = 6
TOTAL = BLOCKS * STEPS
BEFORE = TOTAL - 2
AFTER = TOTAL
GROUP = 8

coupling = 0.6
background = 0.25
phase_unit = math.pi / 32768.0
tan_kappa = math.tan(coupling)
tan_squared = tan_kappa * tan_kappa
end_scale = math.cos(coupling) ** TOTAL / tan_kappa


def passed_along(x, axis, by):
    devices = lax.axis_size(axis)
    return lax.ppermute(x, axis, [(i, (i + by) % devices) for i in range(devices)])


def table_of(step):
    block, last = divmod(step, STEPS)
    return block + (BLOCKS if last == STEPS - 1 else 0)


def sweep_kernel(halves, dests, *refs):
    (inc, before, after, tab_cos, tab_sin, det_cos, det_sin) = refs[:7]
    exit_ref, *int_refs = refs[-5 - halves : -4]
    beam_re, beam_im, bragg_re, bragg_im = refs[-4:]
    span_rows = inc.shape[2] // COLS
    rows = span_rows + BEFORE + AFTER
    dcos = jnp.broadcast_to(det_cos[...], (GROUP, COLS))
    dsin = jnp.broadcast_to(det_sin[...], (GROUP, COLS))

    def at(k):
        return pl.ds(pl.multiple_of(k * COLS, COLS), COLS)

    def turned(re, im, table, row):
        pc = tab_cos[table, pl.ds(row, 1), :]
        ps = tab_sin[table, pl.ds(row, 1), :]
        a = dcos * re + dsin * im
        b = dcos * im - dsin * re
        return pc * a - ps * b, pc * b + ps * a

    def enter(source, count, shift):
        @pl.loop(0, count)
        def _(k):
            re = source[0, :, at(k)]
            im = source[1, :, at(k)]
            beam_re[:, at(k + shift)] = re
            beam_im[:, at(k + shift)] = im
            out_re, out_im = turned(-tan_squared * im, tan_squared * re, table_of(0), k + shift)
            bragg_re[:, at(k + shift)] = out_re
            bragg_im[:, at(k + shift)] = out_im

    enter(before, BEFORE, 0)
    enter(inc, span_rows, BEFORE)
    enter(after, AFTER, BEFORE + span_rows)

    for step in range(1, TOTAL - 1):

        @pl.loop(0, rows // 2 - step)
        def _(pair):
            for odd in range(2):
                k = pair * 2 + odd
                here, there = at(k), at(k + 2 * step)
                t_re, t_im = beam_re[:, here], beam_im[:, here]
                d_re, d_im = bragg_re[:, there], bragg_im[:, there]
                beam_re[:, here] = t_re - d_im
                beam_im[:, here] = t_im + d_re
                out_re, out_im = turned(
                    d_re - tan_squared * t_im, d_im + tan_squared * t_re, table_of(step), k + step
                )
                bragg_re[:, there] = out_re
                bragg_im[:, there] = out_im

    step = TOTAL - 1
    per_dest = span_rows // dests
    per_half = per_dest // halves

    @pl.loop(0, dests)
    def _(dest):
        for inner in range(per_dest):
            k = dest * per_dest + inner
            here, there = at(k), at(k + 2 * step)
            t_re, t_im = beam_re[:, here], beam_im[:, here]
            d_re, d_im = bragg_re[:, there], bragg_im[:, there]
            out_re, out_im = turned(
                d_re - tan_squared * t_im, d_im + tan_squared * t_re, table_of(step), k + step
            )
            exit_ref[0, :, here] = out_re
            exit_ref[1, :, here] = out_im
            half, place = divmod(inner, per_half)
            int_refs[half][dest, :, place * COLS : (place + 1) * COLS] = out_re * out_re + out_im * out_im


def sweep(group, halo, first, halves, dests, count, incident, tables, detune, exit_field, made):
    _, angles, span = incident.shape
    before, after = halo
    rows = span // COLS + BEFORE + AFTER
    points = span // dests // halves
    place = 0 if made is None else made[0]
    whole = lambda x: pl.BlockSpec(x.shape, lambda i: (0,) * x.ndim)
    in_specs = [
        pl.BlockSpec((2, GROUP, span), lambda i: (0, group, 0)),
        pl.BlockSpec((2, GROUP, before.shape[2]), lambda i: (0, group - first, 0)),
        pl.BlockSpec((2, GROUP, after.shape[2]), lambda i: (0, group - first, 0)),
        whole(tables[0]),
        whole(tables[1]),
        pl.BlockSpec((GROUP, 1), lambda i: (group, 0)),
        pl.BlockSpec((GROUP, 1), lambda i: (group, 0)),
    ]
    operands = [incident, before, after, *tables, *detune]
    aliases = {}
    kept = ([] if exit_field is None else [(0, exit_field)]) + (
        [] if made is None else [(1 + half, x) for half, x in enumerate(made[1])]
    )
    for out, x in kept:
        aliases[len(operands)] = out
        in_specs.append(pl.BlockSpec(memory_space=pl.ANY))
        operands.append(x)
    exit_field, *made = pl.pallas_call(
        functools.partial(sweep_kernel, halves, dests),
        grid=(1,),
        out_shape=[jax.ShapeDtypeStruct((2, angles, span), jnp.float32)]
        + [jax.ShapeDtypeStruct((dests, count * GROUP, points), jnp.float32)] * halves,
        in_specs=in_specs,
        out_specs=[pl.BlockSpec((2, GROUP, span), lambda i: (0, group, 0))]
        + [pl.BlockSpec((dests, GROUP, points), lambda i: (0, place, 0))] * halves,
        scratch_shapes=[pltpu.VMEM((GROUP, rows * COLS), jnp.float32)] * 4,
        input_output_aliases=aliases,
        compiler_params=pltpu.CompilerParams(vmem_limit_bytes=40 * 1024 * 1024),
        cost_estimate=pl.CostEstimate(
            flops=20 * TOTAL * GROUP * rows * COLS,
            bytes_accessed=28 * GROUP * span,
            transcendentals=0,
        ),
    )(*operands)
    return exit_field, (place + 1, made)


def place_kernel(half, halves, source, *refs):
    whole, sems = refs[-2:]
    dests, _, part = source.shape
    copies = [
        pltpu.make_async_copy(
            source.at[i], whole.at[:, pl.ds((i * halves + half) * part, part)], sems.at[i]
        )
        for i in range(dests)
    ]
    for copy in copies:
        copy.start()
    for copy in copies:
        copy.wait()


def placed(half, halves, x, whole):
    dests, angles, part = x.shape
    kept = [] if whole is None else [whole]
    return pl.pallas_call(
        functools.partial(place_kernel, half, halves),
        out_shape=jax.ShapeDtypeStruct((angles, dests * halves * part), jnp.float32),
        in_specs=[pl.BlockSpec(memory_space=pl.ANY)] * (1 + len(kept)),
        out_specs=pl.BlockSpec(memory_space=pl.ANY),
        scratch_shapes=[pltpu.SemaphoreType.DMA((dests,))],
        input_output_aliases={1: 0} if kept else {},
        cost_estimate=pl.CostEstimate(flops=0, bytes_accessed=8 * x.size, transcendentals=0),
    )(x, *kept)


def phase_tables(phase):
    earlier = jnp.roll(phase, 1, axis=1)
    leaving = jnp.concatenate([earlier[1:], jnp.zeros_like(phase[:1])], axis=0)
    turns = jnp.concatenate([phase - earlier, phase - leaving], axis=0)
    angle = turns * phase_unit
    scale = jnp.ones((2 * BLOCKS, 1, 1), jnp.float32).at[2 * BLOCKS - 1].set(end_scale)
    return jnp.cos(angle) * scale, jnp.sin(angle) * scale


def deconvolve(response, backward, estimate, counts):
    measured = counts.astype(jnp.float32)
    for _ in range(ITERS):
        blurred = (
            jnp.dot(
                response,
                estimate,
                precision=lax.Precision.HIGH,
                preferred_element_type=jnp.float32,
            )
            + background
        )
        projected = lax.dot_general(
            backward,
            measured / blurred,
            (((0,), (0,)), ((), ())),
            precision=lax.Precision.HIGH,
            preferred_element_type=jnp.float32,
        )
        estimate = estimate * projected
    return estimate


def on_device(incident, detuning, phase_table, response, counts):
    _, angles, span = incident.shape
    dests = lax.axis_size("ang")
    points = span // dests
    halves = 2 if (points // COLS) % 2 == 0 else 1
    part = points // halves
    groups = angles // GROUP

    def neighbours(x):
        return (
            passed_along(x[..., span - BEFORE * COLS :], "lat", 1),
            passed_along(x[..., : AFTER * COLS], "lat", -1),
        )

    def exchanged(x):
        return lax.all_to_all(x, "ang", split_axis=0, concat_axis=0, tiled=True)

    phase = phase_table.astype(jnp.float32)
    ends = (slice(span - BEFORE * COLS, span), slice(0, AFTER * COLS))
    before, after = (
        passed_along(
            jnp.concatenate([incident[0, :GROUP, end], incident[1, :GROUP, end], phase[:, end]]), "lat", by
        )
        for end, by in zip(ends, (1, -1))
    )
    phase = jnp.concatenate([before[2 * GROUP :], phase, after[2 * GROUP :]], axis=1)
    tables = phase_tables(phase.reshape(BLOCKS, -1, COLS))
    halos = {0: (0, tuple(x[: 2 * GROUP].reshape(2, GROUP, -1) for x in (before, after)))}
    group = 1
    while group < groups:
        count = 1
        halo = neighbours(incident[:, group * GROUP : (group + count) * GROUP])
        for one in range(group, group + count):
            halos[one] = (group, halo)
        group += count
    detune = (jnp.cos(detuning)[:, None], jnp.sin(detuning)[:, None])

    lead = max(groups // 2, 1)
    exit_field = made = None
    for group in range(lead):
        first, halo = halos[group]
        exit_field, made = sweep(
            group, halo, first, 1, dests, lead, incident, tables, detune, exit_field, made
        )
    early = exchanged(made[1][0])
    late = []
    if groups > lead:
        made = None
        for group in range(lead, groups):
            first, halo = halos[group]
            exit_field, made = sweep(
                group, halo, first, halves, dests, groups - lead, incident, tables, detune, exit_field, made
            )
        for half in range(halves):
            late.append(exchanged(made[1][half]))
    backward = response / jnp.sum(response, axis=0)[None, :]
    whole = None
    for half in range(halves):
        start = jnp.concatenate(
            [early[:, :, half * part : (half + 1) * part]] + late[half : half + 1], axis=1
        )
        early, start = lax.optimization_barrier((early, start))
        estimate = deconvolve(
            response,
            backward,
            start.reshape(dests * angles, part),
            counts[:, half * part : (half + 1) * part],
        )
        whole = placed(half, halves, exchanged(estimate.reshape(dests, angles, part)), whole)
    return (exit_field, whole)


def solution(mesh):
    return jax.shard_map(
        on_device,
        mesh=mesh,
        in_specs=(P(None, "ang", "lat"), P("ang"), P(None, "lat"), P(), P(None, ("lat", "ang"))),
        out_specs=(P(None, "ang", "lat"), P("ang", "lat")),
        check_vma=False,
    )
```

```python
import functools
import math

import jax
import jax.numpy as jnp
from jax import lax
from jax.experimental import pallas as pl
from jax.experimental.pallas import tpu as pltpu
from jax.sharding import PartitionSpec as P

COLS = 512
BLOCKS = 3
STEPS = 3
ITERS = 6
TOTAL = BLOCKS * STEPS
BEFORE = TOTAL - 2
AFTER = TOTAL
GROUP = 8

coupling = 0.6
background = 0.25
phase_unit = math.pi / 32768.0
tan_kappa = math.tan(coupling)
tan_squared = tan_kappa * tan_kappa
end_scale = math.cos(coupling) ** TOTAL / tan_kappa


def passed_along(x, axis, by):
    devices = lax.axis_size(axis)
    return lax.ppermute(x, axis, [(i, (i + by) % devices) for i in range(devices)])


def table_of(step):
    block, last = divmod(step, STEPS)
    return block + (BLOCKS if last == STEPS - 1 else 0)


def sweep_kernel(halves, dests, *refs):
    (inc, before, after, tab_cos, tab_sin, det_cos, det_sin) = refs[:7]
    exit_ref, *int_refs = refs[-5 - halves : -4]
    beam_re, beam_im, bragg_re, bragg_im = refs[-4:]
    span_rows = inc.shape[2] // COLS
    rows = span_rows + BEFORE + AFTER
    dcos = jnp.broadcast_to(det_cos[...], (GROUP, COLS))
    dsin = jnp.broadcast_to(det_sin[...], (GROUP, COLS))

    def at(k):
        return pl.ds(pl.multiple_of(k * COLS, COLS), COLS)

    def turned(re, im, table, row):
        pc = tab_cos[table, pl.ds(row, 1), :]
        ps = tab_sin[table, pl.ds(row, 1), :]
        a = dcos * re + dsin * im
        b = dcos * im - dsin * re
        return pc * a - ps * b, pc * b + ps * a

    def enter(source, count, shift):
        @pl.loop(0, count)
        def _(k):
            re = source[0, :, at(k)]
            im = source[1, :, at(k)]
            beam_re[:, at(k + shift)] = re
            beam_im[:, at(k + shift)] = im
            out_re, out_im = turned(-tan_squared * im, tan_squared * re, table_of(0), k + shift)
            bragg_re[:, at(k + shift)] = out_re
            bragg_im[:, at(k + shift)] = out_im

    enter(before, BEFORE, 0)
    enter(inc, span_rows, BEFORE)
    enter(after, AFTER, BEFORE + span_rows)

    for step in range(1, TOTAL - 1):

        @pl.loop(0, rows // 2 - step)
        def _(pair):
            for odd in range(2):
                k = pair * 2 + odd
                here, there = at(k), at(k + 2 * step)
                t_re, t_im = beam_re[:, here], beam_im[:, here]
                d_re, d_im = bragg_re[:, there], bragg_im[:, there]
                beam_re[:, here] = t_re - d_im
                beam_im[:, here] = t_im + d_re
                out_re, out_im = turned(
                    d_re - tan_squared * t_im, d_im + tan_squared * t_re, table_of(step), k + step
                )
                bragg_re[:, there] = out_re
                bragg_im[:, there] = out_im

    step = TOTAL - 1
    per_dest = span_rows // dests
    per_half = per_dest // halves

    @pl.loop(0, dests)
    def _(dest):
        for inner in range(per_dest):
            k = dest * per_dest + inner
            here, there = at(k), at(k + 2 * step)
            t_re, t_im = beam_re[:, here], beam_im[:, here]
            d_re, d_im = bragg_re[:, there], bragg_im[:, there]
            out_re, out_im = turned(
                d_re - tan_squared * t_im, d_im + tan_squared * t_re, table_of(step), k + step
            )
            exit_ref[0, :, here] = out_re
            exit_ref[1, :, here] = out_im
            half, place = divmod(inner, per_half)
            int_refs[half][dest, :, place * COLS : (place + 1) * COLS] = out_re * out_re + out_im * out_im


def sweep(group, halo, first, halves, dests, count, incident, tables, detune, exit_field, made):
    _, angles, span = incident.shape
    before, after = halo
    rows = span // COLS + BEFORE + AFTER
    points = span // dests // halves
    place = 0 if made is None else made[0]
    whole = lambda x: pl.BlockSpec(x.shape, lambda i: (0,) * x.ndim)
    in_specs = [
        pl.BlockSpec((2, GROUP, span), lambda i: (0, group, 0)),
        pl.BlockSpec((2, GROUP, before.shape[2]), lambda i: (0, group - first, 0)),
        pl.BlockSpec((2, GROUP, after.shape[2]), lambda i: (0, group - first, 0)),
        whole(tables[0]),
        whole(tables[1]),
        pl.BlockSpec((GROUP, 1), lambda i: (group, 0)),
        pl.BlockSpec((GROUP, 1), lambda i: (group, 0)),
    ]
    operands = [incident, before, after, *tables, *detune]
    aliases = {}
    kept = ([] if exit_field is None else [(0, exit_field)]) + (
        [] if made is None else [(1 + half, x) for half, x in enumerate(made[1])]
    )
    for out, x in kept:
        aliases[len(operands)] = out
        in_specs.append(pl.BlockSpec(memory_space=pl.ANY))
        operands.append(x)
    exit_field, *made = pl.pallas_call(
        functools.partial(sweep_kernel, halves, dests),
        grid=(1,),
        out_shape=[jax.ShapeDtypeStruct((2, angles, span), jnp.float32)]
        + [jax.ShapeDtypeStruct((dests, count * GROUP, points), jnp.float32)] * halves,
        in_specs=in_specs,
        out_specs=[pl.BlockSpec((2, GROUP, span), lambda i: (0, group, 0))]
        + [pl.BlockSpec((dests, GROUP, points), lambda i: (0, place, 0))] * halves,
        scratch_shapes=[pltpu.VMEM((GROUP, rows * COLS), jnp.float32)] * 4,
        input_output_aliases=aliases,
        compiler_params=pltpu.CompilerParams(vmem_limit_bytes=40 * 1024 * 1024),
        cost_estimate=pl.CostEstimate(
            flops=20 * TOTAL * GROUP * rows * COLS,
            bytes_accessed=28 * GROUP * span,
            transcendentals=0,
        ),
    )(*operands)
    return exit_field, (place + 1, made)


def place_kernel(source, *refs):
    refs[-1][...] = source[0]


def placed(half, halves, x, whole):
    dests, angles, part = x.shape
    kept = [] if whole is None else [whole]
    return pl.pallas_call(
        place_kernel,
        grid=(dests,),
        out_shape=jax.ShapeDtypeStruct((angles, dests * halves * part), jnp.float32),
        in_specs=[pl.BlockSpec((1, angles, part), lambda i: (i, 0, 0))]
        + [pl.BlockSpec(memory_space=pl.ANY)] * len(kept),
        out_specs=pl.BlockSpec((angles, part), lambda i: (0, i * halves + half)),
        input_output_aliases={1: 0} if kept else {},
        cost_estimate=pl.CostEstimate(flops=0, bytes_accessed=8 * x.size, transcendentals=0),
    )(x, *kept)


def phase_tables(phase):
    earlier = jnp.roll(phase, 1, axis=1)
    leaving = jnp.concatenate([earlier[1:], jnp.zeros_like(phase[:1])], axis=0)
    turns = jnp.concatenate([phase - earlier, phase - leaving], axis=0)
    angle = turns * phase_unit
    scale = jnp.ones((2 * BLOCKS, 1, 1), jnp.float32).at[2 * BLOCKS - 1].set(end_scale)
    return jnp.cos(angle) * scale, jnp.sin(angle) * scale


def deconvolve(response, backward, estimate, counts):
    measured = counts.astype(jnp.float32)
    for _ in range(ITERS):
        blurred = (
            jnp.dot(
                response,
                estimate,
                precision=lax.Precision.HIGH,
                preferred_element_type=jnp.float32,
            )
            + background
        )
        projected = lax.dot_general(
            backward,
            measured / blurred,
            (((0,), (0,)), ((), ())),
            precision=lax.Precision.HIGH,
            preferred_element_type=jnp.float32,
        )
        estimate = estimate * projected
    return estimate


def on_device(incident, detuning, phase_table, response, counts):
    _, angles, span = incident.shape
    dests = lax.axis_size("ang")
    points = span // dests
    halves = 2 if (points // COLS) % 2 == 0 else 1
    part = points // halves
    groups = angles // GROUP

    def neighbours(x):
        return (
            passed_along(x[..., span - BEFORE * COLS :], "lat", 1),
            passed_along(x[..., : AFTER * COLS], "lat", -1),
        )

    def exchanged(x):
        return lax.all_to_all(x, "ang", split_axis=0, concat_axis=0, tiled=True)

    phase = phase_table.astype(jnp.float32)
    ends = (slice(span - BEFORE * COLS, span), slice(0, AFTER * COLS))
    before, after = (
        passed_along(
            jnp.concatenate([incident[0, :GROUP, end], incident[1, :GROUP, end], phase[:, end]]), "lat", by
        )
        for end, by in zip(ends, (1, -1))
    )
    phase = jnp.concatenate([before[2 * GROUP :], phase, after[2 * GROUP :]], axis=1)
    tables = phase_tables(phase.reshape(BLOCKS, -1, COLS))
    halos = {0: (0, tuple(x[: 2 * GROUP].reshape(2, GROUP, -1) for x in (before, after)))}
    group = 1
    while group < groups:
        count = 1
        halo = neighbours(incident[:, group * GROUP : (group + count) * GROUP])
        for one in range(group, group + count):
            halos[one] = (group, halo)
        group += count
    detune = (jnp.cos(detuning)[:, None], jnp.sin(detuning)[:, None])

    lead = max(groups // 2, 1)
    exit_field = made = None
    for group in range(lead):
        first, halo = halos[group]
        exit_field, made = sweep(
            group, halo, first, 1, dests, lead, incident, tables, detune, exit_field, made
        )
    early = exchanged(made[1][0])
    late = []
    if groups > lead:
        made = None
        for group in range(lead, groups):
            first, halo = halos[group]
            exit_field, made = sweep(
                group, halo, first, halves, dests, groups - lead, incident, tables, detune, exit_field, made
            )
        for half in range(halves):
            late.append(exchanged(made[1][half]))
    backward = response / jnp.sum(response, axis=0)[None, :]
    whole = None
    for half in range(halves):
        start = jnp.concatenate(
            [early[:, :, half * part : (half + 1) * part]] + late[half : half + 1], axis=1
        )
        early, start = lax.optimization_barrier((early, start))
        estimate = deconvolve(
            response,
            backward,
            start.reshape(dests * angles, part),
            counts[:, half * part : (half + 1) * part],
        )
        whole = placed(half, halves, exchanged(estimate.reshape(dests, angles, part)), whole)
    return (exit_field, whole)


def solution(mesh):
    return jax.shard_map(
        on_device,
        mesh=mesh,
        in_specs=(P(None, "ang", "lat"), P("ang"), P(None, "lat"), P(), P(None, ("lat", "ang"))),
        out_specs=(P(None, "ang", "lat"), P("ang", "lat")),
        check_vma=False,
    )
```
